32 devices in a mesh: ctx: 4 (over z), row: 4 (over x, core), col: 2 (over y).
Axes of the slice: x: 2, y: 2, z: 4, core: 2. Of those that a mesh axis runs over, the one named last changes fastest.
Arguments:
- events: bfloat16 [8192, 4096], P(('ctx', 'row'), 'col'), may hold values from -120 to 120
- domain_ids: int32 [8192], P(('ctx', 'row')), may hold values from 0 to 3
- block_order: int32 [4], replicated, may hold values from 0 to 3, each once
- query_weight: bfloat16 [4096, 4096], P('row', 'col'), may hold values from -0.09375 to 0.09375
- keyval_weight: bfloat16 [4096, 8, 2, 128], P('row'), may hold values from -0.09375 to 0.09375
- head_bias: float32 [32], P('col'), may hold values from -1.5 to 1.5
- out_weight: bfloat16 [4096, 4096], P('row', 'col'), may hold values from -0.09375 to 0.09375
Outputs:
- mixed: bfloat16 [8192, 4096], P(('ctx', 'row'), 'col')
The draws below stay inside these ranges and needn't reach their ends.
Inputs may be any that keep to these rules, and one draw needn't show every extreme that they name: `block_order`: each index of ctx holds 2048 consecutive events of one block; every place 0 to 3 is named once.
All inputs are finite; a program needn't handle non-finite values.
Results may differ from the reference program's by a relative error of at most 0.0075.
Values may be sent and summed in bfloat16 or wider, within the bound.
A program may use at most 128 MiB of HBM per device.

```python
import math
import jax
import jax.numpy as jnp
from jax import lax

D = 4096
H = 32
KV = 8
HD = 128
DOMAINS = 4
GROUP_TOK = 2048
TOKENS = 8192
N_CTX = 4


def draw_events(key, part):
    key_base, key_rows, key_cols = jax.random.split(key, 3)
    raw_values = jnp.clip(jax.random.normal(key_base, (TOKENS, D), jnp.float32), -4.0, 4.0)
    row_scale = jnp.exp(jax.random.uniform(key_rows, (TOKENS, 1), jnp.float32, 0.0, math.log(10.0)))
    col_scale = jnp.exp(jax.random.uniform(key_cols, (1, D), jnp.float32, math.log(0.3), math.log(3.0)))
    return (raw_values * row_scale * col_scale).astype(jnp.bfloat16)


def touch_ends(entries, own_key, low, top_value):
    spot = [jax.random.randint(jax.random.fold_in(own_key, axis), (), 0, length) for axis, length in enumerate(entries.shape)]
    longest = entries.shape.index(max(entries.shape))
    next_to = spot[:longest] + [(spot[longest] + 1) % entries.shape[longest]] + spot[longest + 1:]
    return entries.at[tuple(spot)].set(low).at[tuple(next_to)].set(top_value)


def shard_levels(rng, dims, cuts, smallest, top_value):
    level, own = 1.0, jax.random.fold_in(rng, 6)
    for dim, parts in cuts:
        steps = jnp.exp(jax.random.uniform(jax.random.fold_in(own, dim), (parts,), jnp.float32, smallest / len(cuts), top_value / len(cuts)))
        level = level * jnp.repeat(steps, dims[dim] // parts).reshape([-1 if axis == dim else 1 for axis in range(len(dims))])
    return level


def centred(own_key, extent, spread, bound, pieces=(), held_as=jnp.bfloat16):
    values = jax.random.normal(own_key, extent, jnp.float32) * spread
    if len(pieces) > 0:
        values = shard_levels(own_key, extent, pieces, -0.22, 0.18) * values
    return jnp.clip(values, min=-bound, max=bound).astype(held_as)


def setup_inputs(seed: int = 0) -> dict:
    arg_keys = jax.random.split(jax.random.key(seed), 8)
    events = draw_events(jax.random.fold_in(arg_keys[7], 71), 0)
    domain_ids = touch_ends(jax.random.randint(arg_keys[1], (TOKENS,), 0, DOMAINS), jax.random.fold_in(arg_keys[1], 1), 0, DOMAINS - 1).astype(jnp.int32)
    block_order = jax.random.permutation(arg_keys[2], N_CTX).astype(jnp.int32)
    query_weight = centred(arg_keys[3], (D, H * HD), D ** -0.5, 0.09375, ((0, 4), (1, 2)))
    keyval_weight = centred(arg_keys[4], (D, KV, 2, HD), D ** -0.5, 0.09375, ((0, 4),))
    head_bias = jnp.clip(jax.random.uniform(arg_keys[5], (H,), jnp.float32, -1.5, 1.5) * shard_levels(arg_keys[5], (H,), ((0, 2),), -0.4, 0.0), -1.5, 1.5)
    out_weight = centred(arg_keys[6], (H * HD, D), (H * HD) ** -0.5, 0.09375, ((0, 4), (1, 2)))
    return {"events": events, "domain_ids": domain_ids, "block_order": block_order, "query_weight": query_weight, "keyval_weight": keyval_weight, "head_bias": head_bias, "out_weight": out_weight}


norm_eps = 1e-06

def reference(events, domain_ids, block_order, query_weight, keyval_weight, head_bias, out_weight):
    wide_events = events.astype(jnp.float32)
    normed = (wide_events * lax.rsqrt(lax.optimization_barrier(jnp.mean(wide_events * wide_events, axis=1, keepdims=True)) + norm_eps)).astype(jnp.bfloat16)
    queries = jnp.dot(normed, query_weight, preferred_element_type=jnp.float32).astype(jnp.bfloat16)
    queries = queries.reshape(TOKENS, H, HD)
    keyvals = jnp.dot(normed, keyval_weight.reshape(D, KV * 2 * HD), preferred_element_type=jnp.float32).astype(jnp.bfloat16)
    keyvals = keyvals.reshape(TOKENS, KV, 2, HD)
    storage = jnp.arange(TOKENS, dtype=jnp.int32)
    place = block_order[storage // GROUP_TOK] * GROUP_TOK + storage % GROUP_TOK
    inv_count = lax.rsqrt((place + 1).astype(jnp.float32))
    scale_factor = 1.0 / math.sqrt(HD)
    group_size = H // KV

    def one_head(head_index):
        query_head = lax.dynamic_index_in_dim(queries, head_index, 1, keepdims=False)
        pair = lax.dynamic_index_in_dim(keyvals, head_index // group_size, 1, keepdims=False)
        scores = jnp.dot(query_head, pair[:, 0, :].T, preferred_element_type=jnp.float32) * scale_factor
        same_domain = (domain_ids[:, None] == domain_ids[None, :]).astype(jnp.float32)
        scores = scores + lax.dynamic_index_in_dim(head_bias, head_index, 0, keepdims=False) * same_domain
        visible = place[None, :] <= place[:, None]
        weights = jnp.where(visible, jax.nn.silu(scores) * inv_count[:, None], 0.0).astype(jnp.bfloat16)
        return jnp.dot(weights, pair[:, 1, :], preferred_element_type=jnp.float32).astype(jnp.bfloat16)
    per_head = lax.map(one_head, jnp.arange(H, dtype=jnp.int32))
    attended = jnp.transpose(per_head, (1, 0, 2)).reshape(TOKENS, H * HD)
    return jnp.dot(attended, out_weight, preferred_element_type=jnp.float32).astype(jnp.bfloat16)
```

```python
import functools
import math

import jax
import jax.numpy as jnp
from jax import lax
from jax.experimental import pallas as pl
from jax.experimental.pallas import tpu as pltpu
from jax.sharding import PartitionSpec as P

H = 32
KV = 8
HD = 128
LANES = 128
HALF = 32

norm_eps = 1e-06


def block_place(storage, group_rows, block_order):
    block_index = storage // group_rows
    choices_row = jnp.arange(block_order.shape[0], dtype=jnp.int32)
    looked_up = jnp.sum(
        jnp.where(block_index[:, None] == choices_row[None, :], block_order[None, :], 0), axis=1
    )
    return looked_up * group_rows + storage % group_rows


def attention_body(kind_ref, q_ref, kv_ref, qhot_ref, khot_ref, bias_ref, inv_ref, o_ref, qa, ka, acc):
    step = pl.program_id(1)
    group_heads = q_ref.shape[1] // HD
    kind = kind_ref[step]

    @pl.when(step == 0)
    def _():
        acc[...] = jnp.zeros_like(acc)
        for h in range(group_heads):
            qa[h, :, :HD] = q_ref[:, h * HD:(h + 1) * HD]
            qa[h, :, HD:] = (qhot_ref[...] * bias_ref[0, h:h + 1, :]).astype(jnp.bfloat16)

    def tile(diagonal):
        ka[:, :HD] = kv_ref[:, :HD]
        ka[:, HD:] = khot_ref[...]
        for h in range(group_heads):
            half = lax.dot_general(
                qa[h], ka[...], (((1,), (1,)), ((), ())), preferred_element_type=jnp.float32
            )
            w = half * jnp.tanh(half) + half
            if diagonal:
                ti = lax.broadcasted_iota(jnp.int32, w.shape, 0)
                ui = lax.broadcasted_iota(jnp.int32, w.shape, 1)
                w = jnp.where(ui <= ti, w, 0.0)
            acc[h] += jnp.dot(
                w.astype(jnp.bfloat16), kv_ref[:, HD:], preferred_element_type=jnp.float32
            )

    @pl.when(kind == 1)
    def _():
        tile(False)

    @pl.when(kind == 2)
    def _():
        tile(True)

    @pl.when(step == pl.num_programs(1) - 1)
    def _():
        for h in range(group_heads):
            o_ref[:, h * HD:(h + 1) * HD] = (acc[h] * inv_ref[...]).astype(jnp.bfloat16)


def attention(kinds, queries, kv_all, query_hot, key_hot, bias_lanes, inv_count):
    rows, width = queries.shape
    pair_heads, group_heads, _ = bias_lanes.shape
    tiles = kinds.shape[0]
    gw = group_heads * HD
    return pl.pallas_call(
        attention_body,
        grid_spec=pltpu.PrefetchScalarGridSpec(
            num_scalar_prefetch=1,
            grid=(pair_heads, tiles),
            in_specs=[
                pl.BlockSpec((rows, gw), lambda g, j, k: (0, g)),
                pl.BlockSpec((rows, 2 * HD), lambda g, j, k: (j, g)),
                pl.BlockSpec((rows, LANES), lambda g, j, k: (0, 0)),
                pl.BlockSpec((rows, LANES), lambda g, j, k: (j, 0)),
                pl.BlockSpec((1, group_heads, LANES), lambda g, j, k: (g, 0, 0)),
                pl.BlockSpec((rows, 1), lambda g, j, k: (0, 0)),
            ],
            out_specs=pl.BlockSpec((rows, gw), lambda g, j, k: (0, g)),
            scratch_shapes=[
                pltpu.VMEM((group_heads, rows, 2 * HD), jnp.bfloat16),
                pltpu.VMEM((rows, 2 * HD), jnp.bfloat16),
                pltpu.VMEM((group_heads, rows, HD), jnp.float32),
            ],
        ),
        out_shape=jax.ShapeDtypeStruct((rows, width), jnp.bfloat16),
        compiler_params=pltpu.CompilerParams(vmem_limit_bytes=48 * 1024 * 1024),
        cost_estimate=pl.CostEstimate(
            flops=4 * rows * rows * tiles * width, bytes_accessed=rows * tiles * 1024 * 2,
            transcendentals=rows * rows * tiles * width // HD,
        ),
    )(kinds, queries, kv_all, query_hot, key_hot, bias_lanes, inv_count)


def hot_lanes(domains):
    lane = lax.broadcasted_iota(jnp.int32, (1, LANES), 1)
    return ((lane % HALF == domains[:, None]) & (lane < 2 * HALF)).astype(jnp.bfloat16)


def shards(events, domain_ids, block_order, query_weight, keyval_weight, head_bias, out_weight):
    row_count = events.shape[0]
    head_count = head_bias.shape[0]
    group_size = H // KV
    pair_heads = max(1, head_count // group_size)
    group_heads = head_count // pair_heads
    rows_axis = lax.axis_size("row")
    group_rows = row_count * rows_axis
    scale_factor = 1.0 / math.sqrt(HD)
    whole = lax.all_gather(events, "col", axis=1, tiled=True)
    wide_events = whole.astype(jnp.float32)
    normed = (
        wide_events
        * lax.rsqrt(jnp.mean(wide_events * wide_events, axis=1, keepdims=True) + norm_eps)
    ).astype(jnp.bfloat16)
    pair_start = lax.axis_index("col") * head_count // group_size
    pair_weight = lax.dynamic_slice_in_dim(keyval_weight, pair_start, pair_heads, 1)
    pair_weight = pair_weight.reshape(keyval_weight.shape[0], pair_heads * 2 * HD)
    pair_sums = jnp.dot(
        normed,
        lax.all_gather(pair_weight, "row", axis=0, tiled=True),
        preferred_element_type=jnp.float32,
    )
    query_sums = jnp.dot(
        normed,
        lax.all_gather(query_weight, "row", axis=0, tiled=True),
        preferred_element_type=jnp.float32,
    )
    queries = (query_sums * (0.5 * scale_factor)).astype(jnp.bfloat16)
    keyvals = pair_sums.astype(jnp.bfloat16)
    first_row = (lax.axis_index("ctx") * rows_axis + lax.axis_index("row")) * row_count
    query_place = block_place(
        first_row + jnp.arange(row_count, dtype=jnp.int32), group_rows, block_order
    )
    inv_count = lax.rsqrt((query_place + 1).astype(jnp.float32))[:, None]
    half_bias = 0.5 * head_bias
    high = half_bias.astype(jnp.bfloat16).astype(jnp.float32)
    low = half_bias - high
    lane = jnp.arange(LANES, dtype=jnp.int32)[None, :]
    bias_lanes = jnp.where(lane < HALF, high[:, None], jnp.where(lane < 2 * HALF, low[:, None], 0.0))
    bias_lanes = bias_lanes.reshape(pair_heads, group_heads, LANES)
    kv_all = lax.all_gather(keyvals, ("ctx", "row"), axis=0, tiled=True)
    domain_all = lax.all_gather(domain_ids, ("ctx", "row"), axis=0, tiled=True)
    tiles = kv_all.shape[0] // row_count
    tile_first = block_place(
        row_count * jnp.arange(tiles, dtype=jnp.int32), group_rows, block_order
    )
    kinds = jnp.where(
        tile_first < query_place[0], 1, jnp.where(tile_first == query_place[0], 2, 0)
    ).astype(jnp.int32)
    attended = attention(
        kinds, queries, kv_all, hot_lanes(domain_ids), hot_lanes(domain_all), bias_lanes, inv_count
    )
    all_heads = lax.all_gather(attended, "col", axis=1, tiled=True)
    out_sums = jnp.dot(
        all_heads,
        lax.all_gather(out_weight, "row", axis=0, tiled=True),
        preferred_element_type=jnp.float32,
    )
    return out_sums.astype(jnp.bfloat16)


def solution(mesh):
    in_specs = (
        P(("ctx", "row"), "col"),
        P(("ctx", "row")),
        P(),
        P("row", "col"),
        P("row", None, None, None),
        P("col"),
        P("row", "col"),
    )
    out_specs = P(("ctx", "row"), "col")
    return jax.shard_map(shards, mesh=mesh, in_specs=in_specs, out_specs=out_specs, check_vma=False)
```

```python
import functools
import math

import jax
import jax.numpy as jnp
from jax import lax
from jax.experimental import pallas as pl
from jax.experimental.pallas import tpu as pltpu
from jax.sharding import PartitionSpec as P

H = 32
KV = 8
HD = 128
LANES = 128
HALF = 32

norm_eps = 1e-06


def block_place(storage, group_rows, block_order):
    block_index = storage // group_rows
    choices_row = jnp.arange(block_order.shape[0], dtype=jnp.int32)
    looked_up = jnp.sum(
        jnp.where(block_index[:, None] == choices_row[None, :], block_order[None, :], 0), axis=1
    )
    return looked_up * group_rows + storage % group_rows


def attention_body(kind_ref, q_ref, kv_ref, qhot_ref, khot_ref, bias_ref, inv_ref, o_ref, qa, ka, acc):
    step = pl.program_id(1)
    group_heads = q_ref.shape[1] // HD
    kind = kind_ref[step]

    @pl.when(step == 0)
    def _():
        acc[...] = jnp.zeros_like(acc)
        for h in range(group_heads):
            qa[h, :, :HD] = q_ref[:, h * HD:(h + 1) * HD]
            qa[h, :, HD:] = (qhot_ref[...] * bias_ref[0, h:h + 1, :]).astype(jnp.bfloat16)

    def tile(diagonal):
        ka[:, :HD] = kv_ref[:, :HD]
        ka[:, HD:] = khot_ref[...]
        for h in range(group_heads):
            half = lax.dot_general(
                qa[h], ka[...], (((1,), (1,)), ((), ())), preferred_element_type=jnp.float32
            )
            w = half * jnp.tanh(half) + half
            if diagonal:
                ti = lax.broadcasted_iota(jnp.int32, w.shape, 0)
                ui = lax.broadcasted_iota(jnp.int32, w.shape, 1)
                w = jnp.where(ui <= ti, w, 0.0)
            acc[h] += jnp.dot(
                w.astype(jnp.bfloat16), kv_ref[:, HD:], preferred_element_type=jnp.float32
            )

    @pl.when(kind == 1)
    def _():
        tile(False)

    @pl.when(kind == 2)
    def _():
        tile(True)

    @pl.when(step == pl.num_programs(1) - 1)
    def _():
        for h in range(group_heads):
            o_ref[:, h * HD:(h + 1) * HD] = (acc[h] * inv_ref[...]).astype(jnp.bfloat16)


def attention(kinds, queries, kv_all, query_hot, key_hot, bias_lanes, inv_count):
    rows, width = queries.shape
    pair_heads, group_heads, _ = bias_lanes.shape
    tiles = kinds.shape[0]
    gw = group_heads * HD
    return pl.pallas_call(
        attention_body,
        grid_spec=pltpu.PrefetchScalarGridSpec(
            num_scalar_prefetch=1,
            grid=(pair_heads, tiles),
            in_specs=[
                pl.BlockSpec((rows, gw), lambda g, j, k: (0, g)),
                pl.BlockSpec((rows, 2 * HD), lambda g, j, k: (j, g)),
                pl.BlockSpec((rows, LANES), lambda g, j, k: (0, 0)),
                pl.BlockSpec((rows, LANES), lambda g, j, k: (j, 0)),
                pl.BlockSpec((1, group_heads, LANES), lambda g, j, k: (g, 0, 0)),
                pl.BlockSpec((rows, 1), lambda g, j, k: (0, 0)),
            ],
            out_specs=pl.BlockSpec((rows, gw), lambda g, j, k: (0, g)),
            scratch_shapes=[
                pltpu.VMEM((group_heads, rows, 2 * HD), jnp.bfloat16),
                pltpu.VMEM((rows, 2 * HD), jnp.bfloat16),
                pltpu.VMEM((group_heads, rows, HD), jnp.float32),
            ],
        ),
        out_shape=jax.ShapeDtypeStruct((rows, width), jnp.bfloat16),
        compiler_params=pltpu.CompilerParams(vmem_limit_bytes=48 * 1024 * 1024),
        cost_estimate=pl.CostEstimate(
            flops=4 * rows * rows * tiles * width, bytes_accessed=rows * tiles * 1024 * 2,
            transcendentals=rows * rows * tiles * width // HD,
        ),
    )(kinds, queries, kv_all, query_hot, key_hot, bias_lanes, inv_count)


MESH = pl.DeviceIdType.MESH
CHUNKS = 4


def partner(index):
    return index + 1 - 2 * (index % 2)


def weights_body(col_count, n_weights, *refs):
    events = refs[0]
    shards_in = refs[1:1 + n_weights]
    wide = refs[1 + n_weights]
    gathered = refs[2 + n_weights:2 + 2 * n_weights]
    (local_sem, ev_send, ev_recv, x_send, x_recv, z_send, z_recv, o_send, o_recv,
     f_send, f_recv, g_send, g_recv) = refs[2 + 2 * n_weights:]
    z, r, c = lax.axis_index("ctx"), lax.axis_index("row"), lax.axis_index("col")
    mate = {"row": partner(r)}
    across = {"row": (r + 2) % 4}
    beside = {"ctx": partner(z)}
    far = (r + 2) % 4
    mine, other = z % 2, 1 - z % 2

    barrier = pltpu.get_barrier_semaphore()
    peers = [{"col": (c + k) % col_count} for k in range(1, col_count)]
    for peer in [mate, across, beside] + peers:
        pl.semaphore_signal(barrier, inc=1, device_id=peer, device_id_type=MESH)
    pl.semaphore_wait(barrier, 3 + len(peers))

    def remote(src, dst, send, recv, target):
        return pltpu.make_async_remote_copy(
            src_ref=src, dst_ref=dst, send_sem=send, recv_sem=recv,
            device_id=target, device_id_type=MESH,
        )

    width = events.shape[1]
    columns = pl.ds(pl.multiple_of(c * width, 128), width)
    spread = [
        remote(events, wide.at[:, columns], ev_send.at[k], ev_recv.at[k], peer)
        for k, peer in enumerate(peers)
    ]

    def piece(w, half, i):
        size = shards_in[w].shape[0] // (2 * CHUNKS)
        return pl.ds(pl.multiple_of((half * CHUNKS + i) * size, 16), size)

    steps = [(w, i) for w in range(n_weights) for i in range(CHUNKS)]
    cross, relay, over, over_late = [], [], [], []
    for n, (w, i) in enumerate(steps):
        rows, late = piece(w, mine, i), piece(w, other, i)
        out = gathered[w]
        cross.append(remote(
            shards_in[w].at[rows], out.at[r, rows], x_send.at[n], x_recv.at[n], across))
        relay.append(remote(
            out.at[far, rows], out.at[far, rows], z_send.at[n], z_recv.at[n], beside))
        over.append(remote(
            out.at[far, rows], out.at[far, rows], f_send.at[n], f_recv.at[n], mate))
        over_late.append(remote(
            out.at[far, late], out.at[far, late], g_send.at[n], g_recv.at[n], mate))
    own = [
        remote(shards_in[w], gathered[w].at[r], o_send.at[w], o_recv.at[w], mate)
        for w in range(n_weights)
    ]
    keep = [pltpu.make_async_copy(events, wide.at[:, columns], local_sem.at[n_weights])] + [
        pltpu.make_async_copy(shards_in[w], gathered[w].at[r], local_sem.at[w])
        for w in range(n_weights)
    ]
    for copy in cross + spread + own + keep:
        copy.start()
    for n in range(len(steps)):
        cross[n].wait_recv()
        relay[n].start()
        over[n].start()
        if n >= 1:
            relay[n - 1].wait_recv()
            over_late[n - 1].start()
    relay[-1].wait_recv()
    over_late[-1].start()
    for copy in over + over_late + own + spread:
        copy.wait_recv()
    for copy in cross + relay + over + over_late + own + spread:
        copy.wait_send()
    for copy in keep:
        copy.wait()


def gather_weights(col_count, events, weights, name):
    n = len(weights)
    steps = n * CHUNKS
    anywhere = pl.BlockSpec(memory_space=pl.ANY)
    dma = pltpu.SemaphoreType.DMA
    peers = max(1, col_count - 1)
    return pl.pallas_call(
        functools.partial(weights_body, col_count, n),
        out_shape=[jax.ShapeDtypeStruct((events.shape[0], events.shape[1] * col_count), events.dtype)]
        + [jax.ShapeDtypeStruct((4,) + w.shape, w.dtype) for w in weights],
        in_specs=[anywhere] * (1 + n),
        out_specs=[anywhere] * (1 + n),
        scratch_shapes=[dma((n + 1,)), dma((peers,)), dma((peers,)), dma((steps,)), dma((steps,)),
                        dma((steps,)), dma((steps,)), dma((n,)), dma((n,)),
                        dma((steps,)), dma((steps,)), dma((steps,)), dma((steps,))],
        compiler_params=pltpu.CompilerParams(collective_id=name, has_side_effects=True),
    )(events, *weights)


def spread_body(ctx_count, kv, dom, kv_all, dom_all, local_sem,
                up_send, down_send, x_send, c_send, recv_sem):
    z, r = lax.axis_index("ctx"), lax.axis_index("row")
    far, near = (r + 2) % 4, partner(r)
    barrier = pltpu.get_barrier_semaphore()

    def greet(target):
        pl.semaphore_signal(barrier, inc=1, device_id=target, device_id_type=MESH)

    above, below = z < ctx_count - 1, z > 0
    greet({"row": near})
    greet({"row": far})
    pl.when(above)(lambda: greet({"ctx": z + 1}))
    pl.when(below)(lambda: greet({"ctx": z - 1}))
    pl.semaphore_wait(barrier, 2 + (z + ctx_count - 1) // ctx_count + (2 * ctx_count - 2 - z) // ctx_count)

    def copies(zz, rr, send, target, first=False):
        pair = []
        for k, (src, dst) in enumerate(((kv, kv_all), (dom, dom_all))):
            pair.append(pltpu.make_async_remote_copy(
                src_ref=src if first else dst.at[zz, rr], dst_ref=dst.at[zz, rr],
                send_sem=send.at[zz, rr, k] if send is x_send or send is c_send else send.at[zz, k],
                recv_sem=recv_sem.at[zz, rr, k], device_id=target, device_id_type=MESH))
        return pair

    def start(pair):
        for copy in pair:
            copy.start()

    def sent(pair):
        for copy in pair:
            copy.wait_send()

    def landed(zz, rr):
        for copy in copies(zz, rr, x_send, {"row": far}):
            copy.wait_recv()

    keep = [pltpu.make_async_copy(kv, kv_all.at[z, r], local_sem.at[0]),
            pltpu.make_async_copy(dom, dom_all.at[z, r], local_sem.at[1])]

    def up(zz, first=False):
        return copies(zz, r, up_send, {"ctx": z + 1}, first)

    def down(zz, first=False):
        return copies(zz, r, down_send, {"ctx": z - 1}, first)

    def to_far(zz, first=False):
        return copies(zz, r, x_send, {"row": far}, first)

    def to_near(zz, rr, first=False):
        return copies(zz, rr, c_send, {"row": near}, first)

    pl.when(above)(lambda: start(up(z, True)))
    pl.when(below)(lambda: start(down(z, True)))
    start(to_far(z, True))
    start(to_near(z, r, True))
    for copy in keep:
        copy.start()
    landed(z, far)
    start(to_near(z, far))
    for d in range(1, ctx_count):
        @pl.when(z >= d)
        def _():
            landed(z - d, r)
            pl.when(above)(lambda: start(up(z - d)))
            start(to_far(z - d))
            start(to_near(z - d, r))

        @pl.when(z + d < ctx_count)
        def _():
            landed(z + d, r)
            pl.when(below)(lambda: start(down(z + d)))
            start(to_far(z + d))
            start(to_near(z + d, r))

        @pl.when(z >= d)
        def _():
            landed(z - d, far)
            start(to_near(z - d, far))

        @pl.when(z + d < ctx_count)
        def _():
            landed(z + d, far)
            start(to_near(z + d, far))
    mate_far = (near + 2) % 4
    for zz in range(ctx_count):
        landed(zz, near)
        landed(zz, mate_far)
        sent(to_far(zz))
        sent(to_near(zz, r))
        sent(to_near(zz, far))
        pl.when(above & (z >= zz))(lambda zz=zz: sent(up(zz)))
        pl.when(below & (z <= zz))(lambda zz=zz: sent(down(zz)))
    for copy in keep:
        copy.wait()


def gather_keyvals(ctx_count, keyvals, domains, name):
    anywhere = pl.BlockSpec(memory_space=pl.ANY)
    dma = pltpu.SemaphoreType.DMA
    return pl.pallas_call(
        functools.partial(spread_body, ctx_count),
        out_shape=[jax.ShapeDtypeStruct((ctx_count, 4) + keyvals.shape, keyvals.dtype),
                   jax.ShapeDtypeStruct((ctx_count, 4) + domains.shape, domains.dtype)],
        in_specs=[anywhere] * 2,
        out_specs=[anywhere] * 2,
        scratch_shapes=[dma((2,)), dma((ctx_count, 2)), dma((ctx_count, 2)), dma((ctx_count, 4, 2)),
                        dma((ctx_count, 4, 2)), dma((ctx_count, 4, 2))],
        compiler_params=pltpu.CompilerParams(collective_id=name, has_side_effects=True),
    )(keyvals, domains)


def hot_lanes(domains):
    lane = lax.broadcasted_iota(jnp.int32, (1, LANES), 1)
    return ((lane % HALF == domains[:, None]) & (lane < 2 * HALF)).astype(jnp.bfloat16)


def shards(events, domain_ids, block_order, query_weight, keyval_weight, head_bias, out_weight):
    row_count = events.shape[0]
    head_count = head_bias.shape[0]
    group_size = H // KV
    pair_heads = max(1, head_count // group_size)
    group_heads = head_count // pair_heads
    rows_axis = lax.axis_size("row")
    group_rows = row_count * rows_axis
    scale_factor = 1.0 / math.sqrt(HD)
    col_count = lax.axis_size("col")
    pair_start = lax.axis_index("col") * head_count // group_size
    pair_weight = lax.dynamic_slice_in_dim(keyval_weight, pair_start, pair_heads, 1)
    pair_weight = pair_weight.reshape(keyval_weight.shape[0], pair_heads * 2 * HD)
    whole, pair_all, query_all = gather_weights(col_count, events, (pair_weight, query_weight), 1)
    pair_all = pair_all.reshape(-1, pair_all.shape[-1])
    query_all = query_all.reshape(-1, query_all.shape[-1])
    wide_events = whole.astype(jnp.float32)
    normed = (
        wide_events
        * lax.rsqrt(jnp.mean(wide_events * wide_events, axis=1, keepdims=True) + norm_eps)
    ).astype(jnp.bfloat16)
    pair_sums = jnp.dot(
        normed,
        pair_all,
        preferred_element_type=jnp.float32,
    )
    query_sums = jnp.dot(
        normed,
        query_all,
        preferred_element_type=jnp.float32,
    )
    queries = (query_sums * (0.5 * scale_factor)).astype(jnp.bfloat16)
    keyvals = pair_sums.astype(jnp.bfloat16)
    first_row = (lax.axis_index("ctx") * rows_axis + lax.axis_index("row")) * row_count
    query_place = block_place(
        first_row + jnp.arange(row_count, dtype=jnp.int32), group_rows, block_order
    )
    inv_count = lax.rsqrt((query_place + 1).astype(jnp.float32))[:, None]
    half_bias = 0.5 * head_bias
    high = half_bias.astype(jnp.bfloat16).astype(jnp.float32)
    low = half_bias - high
    lane = jnp.arange(LANES, dtype=jnp.int32)[None, :]
    bias_lanes = jnp.where(lane < HALF, high[:, None], jnp.where(lane < 2 * HALF, low[:, None], 0.0))
    bias_lanes = bias_lanes.reshape(pair_heads, group_heads, LANES)
    kv_all, domain_all = gather_keyvals(
        lax.axis_size("ctx"), keyvals, domain_ids.reshape(-1, 128), 2
    )
    kv_all = kv_all.reshape(-1, kv_all.shape[-1])
    domain_all = domain_all.reshape(-1)
    tiles = kv_all.shape[0] // row_count
    tile_first = block_place(
        row_count * jnp.arange(tiles, dtype=jnp.int32), group_rows, block_order
    )
    kinds = jnp.where(
        tile_first < query_place[0], 1, jnp.where(tile_first == query_place[0], 2, 0)
    ).astype(jnp.int32)
    attended = attention(
        kinds, queries, kv_all, hot_lanes(domain_ids), hot_lanes(domain_all), bias_lanes, inv_count
    )
    all_heads = lax.all_gather(attended, "col", axis=1, tiled=True)
    out_sums = jnp.dot(
        all_heads,
        lax.all_gather(out_weight, "row", axis=0, tiled=True),
        preferred_element_type=jnp.float32,
    )
    return out_sums.astype(jnp.bfloat16)


def solution(mesh):
    in_specs = (
        P(("ctx", "row"), "col"),
        P(("ctx", "row")),
        P(),
        P("row", "col"),
        P("row", None, None, None),
        P("col"),
        P("row", "col"),
    )
    out_specs = P(("ctx", "row"), "col")
    return jax.shard_map(shards, mesh=mesh, in_specs=in_specs, out_specs=out_specs, check_vma=False)
```

```python
import functools
import math

import jax
import jax.numpy as jnp
from jax import lax
from jax.experimental import pallas as pl
from jax.experimental.pallas import tpu as pltpu
from jax.sharding import PartitionSpec as P

H = 32
KV = 8
HD = 128
LANES = 128
HALF = 32

norm_eps = 1e-06


def block_place(storage, group_rows, block_order):
    block_index = storage // group_rows
    choices_row = jnp.arange(block_order.shape[0], dtype=jnp.int32)
    looked_up = jnp.sum(
        jnp.where(block_index[:, None] == choices_row[None, :], block_order[None, :], 0), axis=1
    )
    return looked_up * group_rows + storage % group_rows


def attention_body(kind_ref, q_ref, kv_ref, qhot_ref, khot_ref, bias_ref, inv_ref, o_ref, qa, ka, acc):
    step = pl.program_id(1)
    group_heads = q_ref.shape[1] // HD
    kind = kind_ref[step]

    @pl.when(step == 0)
    def _():
        acc[...] = jnp.zeros_like(acc)
        for h in range(group_heads):
            qa[h, :, :HD] = q_ref[:, h * HD:(h + 1) * HD]
            qa[h, :, HD:] = (qhot_ref[...] * bias_ref[0, h:h + 1, :]).astype(jnp.bfloat16)

    def tile(diagonal):
        ka[:, :HD] = kv_ref[:, :HD]
        ka[:, HD:] = khot_ref[...]
        for h in range(group_heads):
            half = lax.dot_general(
                qa[h], ka[...], (((1,), (1,)), ((), ())), preferred_element_type=jnp.float32
            )
            w = half * jnp.tanh(half) + half
            if diagonal:
                ti = lax.broadcasted_iota(jnp.int32, w.shape, 0)
                ui = lax.broadcasted_iota(jnp.int32, w.shape, 1)
                w = jnp.where(ui <= ti, w, 0.0)
            acc[h] += jnp.dot(
                w.astype(jnp.bfloat16), kv_ref[:, HD:], preferred_element_type=jnp.float32
            )

    @pl.when(kind == 1)
    def _():
        tile(False)

    @pl.when(kind == 2)
    def _():
        tile(True)

    @pl.when(step == pl.num_programs(1) - 1)
    def _():
        for h in range(group_heads):
            o_ref[:, h * HD:(h + 1) * HD] = (acc[h] * inv_ref[...]).astype(jnp.bfloat16)


def attention(kinds, queries, kv_all, query_hot, key_hot, bias_lanes, inv_count):
    rows, width = queries.shape
    pair_heads, group_heads, _ = bias_lanes.shape
    tiles = kinds.shape[0]
    gw = group_heads * HD
    return pl.pallas_call(
        attention_body,
        grid_spec=pltpu.PrefetchScalarGridSpec(
            num_scalar_prefetch=1,
            grid=(pair_heads, tiles),
            in_specs=[
                pl.BlockSpec((rows, gw), lambda g, j, k: (0, g)),
                pl.BlockSpec((rows, 2 * HD), lambda g, j, k: (j, g)),
                pl.BlockSpec((rows, LANES), lambda g, j, k: (0, 0)),
                pl.BlockSpec((rows, LANES), lambda g, j, k: (j, 0)),
                pl.BlockSpec((1, group_heads, LANES), lambda g, j, k: (g, 0, 0)),
                pl.BlockSpec((rows, 1), lambda g, j, k: (0, 0)),
            ],
            out_specs=pl.BlockSpec((rows, gw), lambda g, j, k: (0, g)),
            scratch_shapes=[
                pltpu.VMEM((group_heads, rows, 2 * HD), jnp.bfloat16),
                pltpu.VMEM((rows, 2 * HD), jnp.bfloat16),
                pltpu.VMEM((group_heads, rows, HD), jnp.float32),
            ],
        ),
        out_shape=jax.ShapeDtypeStruct((rows, width), jnp.bfloat16),
        compiler_params=pltpu.CompilerParams(vmem_limit_bytes=48 * 1024 * 1024),
        cost_estimate=pl.CostEstimate(
            flops=4 * rows * rows * tiles * width, bytes_accessed=rows * tiles * 1024 * 2,
            transcendentals=rows * rows * tiles * width // HD,
        ),
    )(kinds, queries, kv_all, query_hot, key_hot, bias_lanes, inv_count)


MESH = pl.DeviceIdType.MESH
CHUNKS = 4


def partner(index):
    return index + 1 - 2 * (index % 2)


def columns_body(col_count, part, wide, local_sem, send, recv):
    c = lax.axis_index("col")
    peers = [{"col": (c + k) % col_count} for k in range(1, col_count)]
    barrier = pltpu.get_barrier_semaphore()
    for peer in peers:
        pl.semaphore_signal(barrier, inc=1, device_id=peer, device_id_type=MESH)
    pl.semaphore_wait(barrier, len(peers))
    width = part.shape[1]
    size = part.shape[0] // CHUNKS
    columns = pl.ds(pl.multiple_of(c * width, 128), width)
    copies = []
    for i in range(CHUNKS):
        rows = pl.ds(i * size, size)
        for k, peer in enumerate(peers):
            copies.append(pltpu.make_async_remote_copy(
                src_ref=part.at[rows], dst_ref=wide.at[rows, columns],
                send_sem=send.at[k, i], recv_sem=recv.at[k, i],
                device_id=peer, device_id_type=MESH))
    keep = pltpu.make_async_copy(part, wide.at[:, columns], local_sem)
    for copy in copies:
        copy.start()
    keep.start()
    for copy in copies:
        copy.wait()
    keep.wait()


def gather_columns(col_count, part, name):
    dma = pltpu.SemaphoreType.DMA
    return pl.pallas_call(
        functools.partial(columns_body, col_count),
        out_shape=jax.ShapeDtypeStruct((part.shape[0], part.shape[1] * col_count), part.dtype),
        in_specs=[pl.BlockSpec(memory_space=pltpu.VMEM)],
        out_specs=pl.BlockSpec(memory_space=pl.ANY),
        scratch_shapes=[dma, dma((col_count - 1, CHUNKS)), dma((col_count - 1, CHUNKS))],
        compiler_params=pltpu.CompilerParams(
            collective_id=name, has_side_effects=True, vmem_limit_bytes=16 * 1024 * 1024),
        cost_estimate=pl.CostEstimate(
            flops=0, bytes_accessed=32 * part.size * 2, transcendentals=0),
    )(part)


def spread_body(ctx_count, kv, dom, kv_all, dom_all, local_sem,
                up_send, down_send, x_send, c_send, recv_sem):
    z, r = lax.axis_index("ctx"), lax.axis_index("row")
    far, near = (r + 2) % 4, partner(r)
    barrier = pltpu.get_barrier_semaphore()

    def greet(target):
        pl.semaphore_signal(barrier, inc=1, device_id=target, device_id_type=MESH)

    above, below = z < ctx_count - 1, z > 0
    greet({"row": near})
    greet({"row": far})
    pl.when(above)(lambda: greet({"ctx": z + 1}))
    pl.when(below)(lambda: greet({"ctx": z - 1}))
    pl.semaphore_wait(barrier, 2 + (z + ctx_count - 1) // ctx_count + (2 * ctx_count - 2 - z) // ctx_count)

    def copies(zz, rr, send, target, first=False):
        pair = []
        for k, (src, dst) in enumerate(((kv, kv_all), (dom, dom_all))):
            pair.append(pltpu.make_async_remote_copy(
                src_ref=src if first else dst.at[zz, rr], dst_ref=dst.at[zz, rr],
                send_sem=send.at[zz, rr, k] if send is x_send or send is c_send else send.at[zz, k],
                recv_sem=recv_sem.at[zz, rr, k], device_id=target, device_id_type=MESH))
        return pair

    def start(pair):
        for copy in pair:
            copy.start()

    def sent(pair):
        for copy in pair:
            copy.wait_send()

    def landed(zz, rr):
        for copy in copies(zz, rr, x_send, {"row": far}):
            copy.wait_recv()

    keep = [pltpu.make_async_copy(kv, kv_all.at[z, r], local_sem.at[0]),
            pltpu.make_async_copy(dom, dom_all.at[z, r], local_sem.at[1])]

    def up(zz, first=False):
        return copies(zz, r, up_send, {"ctx": z + 1}, first)

    def down(zz, first=False):
        return copies(zz, r, down_send, {"ctx": z - 1}, first)

    def to_far(zz, first=False):
        return copies(zz, r, x_send, {"row": far}, first)

    def to_near(zz, rr, first=False):
        return copies(zz, rr, c_send, {"row": near}, first)

    pl.when(above)(lambda: start(up(z, True)))
    pl.when(below)(lambda: start(down(z, True)))
    start(to_far(z, True))
    start(to_near(z, r, True))
    for copy in keep:
        copy.start()
    landed(z, far)
    start(to_near(z, far))
    for d in range(1, ctx_count):
        @pl.when(z >= d)
        def _():
            landed(z - d, r)
            pl.when(above)(lambda: start(up(z - d)))
            start(to_far(z - d))
            start(to_near(z - d, r))

        @pl.when(z + d < ctx_count)
        def _():
            landed(z + d, r)
            pl.when(below)(lambda: start(down(z + d)))
            start(to_far(z + d))
            start(to_near(z + d, r))

        @pl.when(z >= d)
        def _():
            landed(z - d, far)
            start(to_near(z - d, far))

        @pl.when(z + d < ctx_count)
        def _():
            landed(z + d, far)
            start(to_near(z + d, far))
    mate_far = (near + 2) % 4
    for zz in range(ctx_count):
        landed(zz, near)
        landed(zz, mate_far)
        sent(to_far(zz))
        sent(to_near(zz, r))
        sent(to_near(zz, far))
        pl.when(above & (z >= zz))(lambda zz=zz: sent(up(zz)))
        pl.when(below & (z <= zz))(lambda zz=zz: sent(down(zz)))
    for copy in keep:
        copy.wait()


def gather_keyvals(ctx_count, keyvals, domains, name):
    anywhere = pl.BlockSpec(memory_space=pl.ANY)
    dma = pltpu.SemaphoreType.DMA
    return pl.pallas_call(
        functools.partial(spread_body, ctx_count),
        out_shape=[jax.ShapeDtypeStruct((ctx_count, 4) + keyvals.shape, keyvals.dtype),
                   jax.ShapeDtypeStruct((ctx_count, 4) + domains.shape, domains.dtype)],
        in_specs=[pl.BlockSpec(memory_space=pltpu.VMEM)] * 2,
        out_specs=[anywhere] * 2,
        scratch_shapes=[dma((2,)), dma((ctx_count, 2)), dma((ctx_count, 2)), dma((ctx_count, 4, 2)),
                        dma((ctx_count, 4, 2)), dma((ctx_count, 4, 2))],
        compiler_params=pltpu.CompilerParams(collective_id=name, has_side_effects=True,
                                             vmem_limit_bytes=16 * 1024 * 1024),
        cost_estimate=pl.CostEstimate(
            flops=0, bytes_accessed=128 * keyvals.size * 2, transcendentals=0),
    )(keyvals, domains)


def hot_lanes(domains):
    lane = lax.broadcasted_iota(jnp.int32, (1, LANES), 1)
    return ((lane % HALF == domains[:, None]) & (lane < 2 * HALF)).astype(jnp.bfloat16)


def shards(events, domain_ids, block_order, query_weight, keyval_weight, head_bias, out_weight):
    row_count = events.shape[0]
    head_count = head_bias.shape[0]
    group_size = H // KV
    pair_heads = max(1, head_count // group_size)
    group_heads = head_count // pair_heads
    rows_axis = lax.axis_size("row")
    group_rows = row_count * rows_axis
    scale_factor = 1.0 / math.sqrt(HD)
    col_count = lax.axis_size("col")
    pair_start = lax.axis_index("col") * head_count // group_size
    pair_weight = lax.dynamic_slice_in_dim(keyval_weight, pair_start, pair_heads, 1)
    pair_weight = pair_weight.reshape(keyval_weight.shape[0], pair_heads * 2 * HD)
    pair_all = lax.all_gather(pair_weight, "row", axis=0, tiled=True)
    query_all = lax.all_gather(query_weight, "row", axis=0, tiled=True)
    whole = gather_columns(col_count, events, 1)
    wide_events = whole.astype(jnp.float32)
    normed = (
        wide_events
        * lax.rsqrt(jnp.mean(wide_events * wide_events, axis=1, keepdims=True) + norm_eps)
    ).astype(jnp.bfloat16)
    pair_sums = jnp.dot(
        normed,
        pair_all,
        preferred_element_type=jnp.float32,
    )
    query_sums = jnp.dot(
        normed,
        query_all,
        preferred_element_type=jnp.float32,
    )
    queries = (query_sums * (0.5 * scale_factor)).astype(jnp.bfloat16)
    keyvals = pair_sums.astype(jnp.bfloat16)
    first_row = (lax.axis_index("ctx") * rows_axis + lax.axis_index("row")) * row_count
    query_place = block_place(
        first_row + jnp.arange(row_count, dtype=jnp.int32), group_rows, block_order
    )
    inv_count = lax.rsqrt((query_place + 1).astype(jnp.float32))[:, None]
    half_bias = 0.5 * head_bias
    high = half_bias.astype(jnp.bfloat16).astype(jnp.float32)
    low = half_bias - high
    lane = jnp.arange(LANES, dtype=jnp.int32)[None, :]
    bias_lanes = jnp.where(lane < HALF, high[:, None], jnp.where(lane < 2 * HALF, low[:, None], 0.0))
    bias_lanes = bias_lanes.reshape(pair_heads, group_heads, LANES)
    kv_all, domain_all = gather_keyvals(
        lax.axis_size("ctx"), keyvals, domain_ids.reshape(-1, 128), 2
    )
    kv_all = kv_all.reshape(-1, kv_all.shape[-1])
    domain_all = domain_all.reshape(-1)
    tiles = kv_all.shape[0] // row_count
    tile_first = block_place(
        row_count * jnp.arange(tiles, dtype=jnp.int32), group_rows, block_order
    )
    kinds = jnp.where(
        tile_first < query_place[0], 1, jnp.where(tile_first == query_place[0], 2, 0)
    ).astype(jnp.int32)
    attended = attention(
        kinds, queries, kv_all, hot_lanes(domain_ids), hot_lanes(domain_all), bias_lanes, inv_count
    )
    all_heads = gather_columns(col_count, attended, 3)
    out_sums = jnp.dot(
        all_heads,
        lax.all_gather(out_weight, "row", axis=0, tiled=True),
        preferred_element_type=jnp.float32,
    )
    return out_sums.astype(jnp.bfloat16)


def solution(mesh):
    in_specs = (
        P(("ctx", "row"), "col"),
        P(("ctx", "row")),
        P(),
        P("row", "col"),
        P("row", None, None, None),
        P("col"),
        P("row", "col"),
    )
    out_specs = P(("ctx", "row"), "col")
    return jax.shard_map(shards, mesh=mesh, in_specs=in_specs, out_specs=out_specs, check_vma=False)
```

```python
import functools
import math

import jax
import jax.numpy as jnp
from jax import lax
from jax.experimental import pallas as pl
from jax.experimental.pallas import tpu as pltpu
from jax.sharding import PartitionSpec as P

H = 32
KV = 8
HD = 128
LANES = 128
HALF = 32

norm_eps = 1e-06


def block_place(storage, group_rows, block_order):
    block_index = storage // group_rows
    choices_row = jnp.arange(block_order.shape[0], dtype=jnp.int32)
    looked_up = jnp.sum(
        jnp.where(block_index[:, None] == choices_row[None, :], block_order[None, :], 0), axis=1
    )
    return looked_up * group_rows + storage % group_rows


def attention_body(kind_ref, q_ref, kv_ref, qhot_ref, khot_ref, bias_ref, inv_ref, o_ref, qa, ka, acc):
    step = pl.program_id(1)
    group_heads = q_ref.shape[1] // HD
    kind = kind_ref[step]

    @pl.when(step == 0)
    def _():
        acc[...] = jnp.zeros_like(acc)
        for h in range(group_heads):
            qa[h, :, :HD] = q_ref[:, h * HD:(h + 1) * HD]
            qa[h, :, HD:] = (qhot_ref[...] * bias_ref[0, h:h + 1, :]).astype(jnp.bfloat16)

    def tile(diagonal):
        ka[:, :HD] = kv_ref[:, :HD]
        ka[:, HD:] = khot_ref[...]
        for h in range(group_heads):
            half = lax.dot_general(
                qa[h], ka[...], (((1,), (1,)), ((), ())), preferred_element_type=jnp.float32
            )
            w = half * jnp.tanh(half) + half
            if diagonal:
                ti = lax.broadcasted_iota(jnp.int32, w.shape, 0)
                ui = lax.broadcasted_iota(jnp.int32, w.shape, 1)
                w = jnp.where(ui <= ti, w, 0.0)
            acc[h] += jnp.dot(
                w.astype(jnp.bfloat16), kv_ref[:, HD:], preferred_element_type=jnp.float32
            )

    @pl.when(kind == 1)
    def _():
        tile(False)

    @pl.when(kind == 2)
    def _():
        tile(True)

    @pl.when(step == pl.num_programs(1) - 1)
    def _():
        for h in range(group_heads):
            o_ref[:, h * HD:(h + 1) * HD] = (acc[h] * inv_ref[...]).astype(jnp.bfloat16)


def attention(kinds, queries, kv_all, query_hot, key_hot, bias_lanes, inv_count):
    rows, width = queries.shape
    pair_heads, group_heads, _ = bias_lanes.shape
    tiles = kinds.shape[0]
    gw = group_heads * HD
    return pl.pallas_call(
        attention_body,
        grid_spec=pltpu.PrefetchScalarGridSpec(
            num_scalar_prefetch=1,
            grid=(pair_heads, tiles),
            in_specs=[
                pl.BlockSpec((rows, gw), lambda g, j, k: (0, g)),
                pl.BlockSpec((rows, 2 * HD), lambda g, j, k: (j, g)),
                pl.BlockSpec((rows, LANES), lambda g, j, k: (0, 0)),
                pl.BlockSpec((rows, LANES), lambda g, j, k: (j, 0)),
                pl.BlockSpec((1, group_heads, LANES), lambda g, j, k: (g, 0, 0)),
                pl.BlockSpec((rows, 1), lambda g, j, k: (0, 0)),
            ],
            out_specs=pl.BlockSpec((rows, gw), lambda g, j, k: (0, g)),
            scratch_shapes=[
                pltpu.VMEM((group_heads, rows, 2 * HD), jnp.bfloat16),
                pltpu.VMEM((rows, 2 * HD), jnp.bfloat16),
                pltpu.VMEM((group_heads, rows, HD), jnp.float32),
            ],
        ),
        out_shape=jax.ShapeDtypeStruct((rows, width), jnp.bfloat16),
        compiler_params=pltpu.CompilerParams(vmem_limit_bytes=48 * 1024 * 1024),
        cost_estimate=pl.CostEstimate(
            flops=4 * rows * rows * tiles * width, bytes_accessed=rows * tiles * 1024 * 2,
            transcendentals=rows * rows * tiles * width // HD,
        ),
    )(kinds, queries, kv_all, query_hot, key_hot, bias_lanes, inv_count)


MESH = pl.DeviceIdType.MESH
CHUNKS = 4


def partner(index):
    return index + 1 - 2 * (index % 2)


def columns_body(col_count, part, wide, local_sem, send, recv):
    c = lax.axis_index("col")
    peers = [{"col": (c + k) % col_count} for k in range(1, col_count)]
    barrier = pltpu.get_barrier_semaphore()
    for peer in peers:
        pl.semaphore_signal(barrier, inc=1, device_id=peer, device_id_type=MESH)
    pl.semaphore_wait(barrier, len(peers))
    width = part.shape[1]
    size = part.shape[0] // CHUNKS
    columns = pl.ds(pl.multiple_of(c * width, 128), width)
    copies = []
    for i in range(CHUNKS):
        rows = pl.ds(i * size, size)
        for k, peer in enumerate(peers):
            copies.append(pltpu.make_async_remote_copy(
                src_ref=part.at[rows], dst_ref=wide.at[rows, columns],
                send_sem=send.at[k, i], recv_sem=recv.at[k, i],
                device_id=peer, device_id_type=MESH))
    keep = pltpu.make_async_copy(part, wide.at[:, columns], local_sem)
    for copy in copies:
        copy.start()
    keep.start()
    for copy in copies:
        copy.wait()
    keep.wait()


def gather_columns(col_count, part, name):
    dma = pltpu.SemaphoreType.DMA
    return pl.pallas_call(
        functools.partial(columns_body, col_count),
        out_shape=jax.ShapeDtypeStruct((part.shape[0], part.shape[1] * col_count), part.dtype),
        in_specs=[pl.BlockSpec(memory_space=pltpu.VMEM)],
        out_specs=pl.BlockSpec(memory_space=pl.ANY),
        scratch_shapes=[dma, dma((col_count - 1, CHUNKS)), dma((col_count - 1, CHUNKS))],
        compiler_params=pltpu.CompilerParams(
            collective_id=name, has_side_effects=True, vmem_limit_bytes=16 * 1024 * 1024),
        cost_estimate=pl.CostEstimate(
            flops=0, bytes_accessed=32 * part.size * 2, transcendentals=0),
    )(part)


def spread_body(ctx_count, kv, dom, kv_all, dom_all, local_sem,
                up_send, down_send, x_send, c_send, recv_sem):
    z, r = lax.axis_index("ctx"), lax.axis_index("row")
    far, near = (r + 2) % 4, partner(r)
    barrier = pltpu.get_barrier_semaphore()

    def greet(target):
        pl.semaphore_signal(barrier, inc=1, device_id=target, device_id_type=MESH)

    above, below = z < ctx_count - 1, z > 0
    greet({"row": near})
    greet({"row": far})
    pl.when(above)(lambda: greet({"ctx": z + 1}))
    pl.when(below)(lambda: greet({"ctx": z - 1}))
    pl.semaphore_wait(barrier, 2 + (z + ctx_count - 1) // ctx_count + (2 * ctx_count - 2 - z) // ctx_count)

    def copies(zz, rr, send, target, first=False):
        pair = []
        for k, (src, dst) in enumerate(((kv, kv_all), (dom, dom_all))):
            pair.append(pltpu.make_async_remote_copy(
                src_ref=src if first else dst.at[zz, rr], dst_ref=dst.at[zz, rr],
                send_sem=send.at[zz, rr, k],
                recv_sem=recv_sem.at[zz, rr, k], device_id=target, device_id_type=MESH))
        return pair

    def start(pair):
        for copy in pair:
            copy.start()

    def sent(pair):
        for copy in pair:
            copy.wait_send()

    def landed(zz, rr):
        for copy in copies(zz, rr, x_send, {"row": far}):
            copy.wait_recv()

    keep = [pltpu.make_async_copy(kv, kv_all.at[z, r], local_sem.at[0]),
            pltpu.make_async_copy(dom, dom_all.at[z, r], local_sem.at[1])]

    def up(zz, rr, first=False):
        return copies(zz, rr, up_send, {"ctx": z + 1}, first)

    def down(zz, rr, first=False):
        return copies(zz, rr, down_send, {"ctx": z - 1}, first)

    def to_near(zz, rr, first=False):
        return copies(zz, rr, c_send, {"row": near}, first)

    across = copies(z, r, x_send, {"row": far}, True)
    start(across)
    pl.when(above)(lambda: start(up(z, r, True)))
    pl.when(below)(lambda: start(down(z, r, True)))
    start(to_near(z, r, True))
    for copy in keep:
        copy.start()
    landed(z, far)
    pl.when(above)(lambda: start(up(z, far)))
    pl.when(below)(lambda: start(down(z, far)))
    start(to_near(z, far))
    for d in range(1, ctx_count):
        for rr in (r, far):
            @pl.when(z >= d)
            def _():
                landed(z - d, rr)
                pl.when(above)(lambda: start(up(z - d, rr)))
                start(to_near(z - d, rr))

            @pl.when(z + d < ctx_count)
            def _():
                landed(z + d, rr)
                pl.when(below)(lambda: start(down(z + d, rr)))
                start(to_near(z + d, rr))

    sent(across)
    for zz in range(ctx_count):
        landed(zz, near)
        landed(zz, (near + 2) % 4)
        for rr in (r, far):
            sent(to_near(zz, rr))
            pl.when(above & (z >= zz))(lambda zz=zz, rr=rr: sent(up(zz, rr)))
            pl.when(below & (z <= zz))(lambda zz=zz, rr=rr: sent(down(zz, rr)))
    for copy in keep:
        copy.wait()


def gather_keyvals(ctx_count, keyvals, domains, name):
    anywhere = pl.BlockSpec(memory_space=pl.ANY)
    dma = pltpu.SemaphoreType.DMA
    return pl.pallas_call(
        functools.partial(spread_body, ctx_count),
        out_shape=[jax.ShapeDtypeStruct((ctx_count, 4) + keyvals.shape, keyvals.dtype),
                   jax.ShapeDtypeStruct((ctx_count, 4) + domains.shape, domains.dtype)],
        in_specs=[pl.BlockSpec(memory_space=pltpu.VMEM)] * 2,
        out_specs=[anywhere] * 2,
        scratch_shapes=[dma((2,)), dma((ctx_count, 4, 2)), dma((ctx_count, 4, 2)), dma((ctx_count, 4, 2)),
                        dma((ctx_count, 4, 2)), dma((ctx_count, 4, 2))],
        compiler_params=pltpu.CompilerParams(collective_id=name, has_side_effects=True,
                                             vmem_limit_bytes=16 * 1024 * 1024),
        cost_estimate=pl.CostEstimate(
            flops=0, bytes_accessed=128 * keyvals.size * 2, transcendentals=0),
    )(keyvals, domains)


def hot_lanes(domains):
    lane = lax.broadcasted_iota(jnp.int32, (1, LANES), 1)
    return ((lane % HALF == domains[:, None]) & (lane < 2 * HALF)).astype(jnp.bfloat16)


def shards(events, domain_ids, block_order, query_weight, keyval_weight, head_bias, out_weight):
    row_count = events.shape[0]
    head_count = head_bias.shape[0]
    group_size = H // KV
    pair_heads = max(1, head_count // group_size)
    group_heads = head_count // pair_heads
    rows_axis = lax.axis_size("row")
    group_rows = row_count * rows_axis
    scale_factor = 1.0 / math.sqrt(HD)
    col_count = lax.axis_size("col")
    pair_start = lax.axis_index("col") * head_count // group_size
    pair_weight = lax.dynamic_slice_in_dim(keyval_weight, pair_start, pair_heads, 1)
    pair_weight = pair_weight.reshape(keyval_weight.shape[0], pair_heads * 2 * HD)
    pair_all = lax.all_gather(pair_weight, "row", axis=0, tiled=True)
    query_all = lax.all_gather(query_weight, "row", axis=0, tiled=True)
    whole = gather_columns(col_count, events, 1)
    wide_events = whole.astype(jnp.float32)
    normed = (
        wide_events
        * lax.rsqrt(jnp.mean(wide_events * wide_events, axis=1, keepdims=True) + norm_eps)
    ).astype(jnp.bfloat16)
    pair_sums = jnp.dot(
        normed,
        pair_all,
        preferred_element_type=jnp.float32,
    )
    query_sums = jnp.dot(
        normed,
        query_all,
        preferred_element_type=jnp.float32,
    )
    queries = (query_sums * (0.5 * scale_factor)).astype(jnp.bfloat16)
    keyvals = pair_sums.astype(jnp.bfloat16)
    first_row = (lax.axis_index("ctx") * rows_axis + lax.axis_index("row")) * row_count
    query_place = block_place(
        first_row + jnp.arange(row_count, dtype=jnp.int32), group_rows, block_order
    )
    inv_count = lax.rsqrt((query_place + 1).astype(jnp.float32))[:, None]
    half_bias = 0.5 * head_bias
    high = half_bias.astype(jnp.bfloat16).astype(jnp.float32)
    low = half_bias - high
    lane = jnp.arange(LANES, dtype=jnp.int32)[None, :]
    bias_lanes = jnp.where(lane < HALF, high[:, None], jnp.where(lane < 2 * HALF, low[:, None], 0.0))
    bias_lanes = bias_lanes.reshape(pair_heads, group_heads, LANES)
    kv_all, domain_all = gather_keyvals(
        lax.axis_size("ctx"), keyvals, domain_ids.reshape(-1, 128), 2
    )
    kv_all = kv_all.reshape(-1, kv_all.shape[-1])
    domain_all = domain_all.reshape(-1)
    tiles = kv_all.shape[0] // row_count
    tile_first = block_place(
        row_count * jnp.arange(tiles, dtype=jnp.int32), group_rows, block_order
    )
    kinds = jnp.where(
        tile_first < query_place[0], 1, jnp.where(tile_first == query_place[0], 2, 0)
    ).astype(jnp.int32)
    attended = attention(
        kinds, queries, kv_all, hot_lanes(domain_ids), hot_lanes(domain_all), bias_lanes, inv_count
    )
    all_heads = gather_columns(col_count, attended, 3)
    out_sums = jnp.dot(
        all_heads,
        lax.all_gather(out_weight, "row", axis=0, tiled=True),
        preferred_element_type=jnp.float32,
    )
    return out_sums.astype(jnp.bfloat16)


def solution(mesh):
    in_specs = (
        P(("ctx", "row"), "col"),
        P(("ctx", "row")),
        P(),
        P("row", "col"),
        P("row", None, None, None),
        P("col"),
        P("row", "col"),
    )
    out_specs = P(("ctx", "row"), "col")
    return jax.shard_map(shards, mesh=mesh, in_specs=in_specs, out_specs=out_specs, check_vma=False)
```

```python
import functools
import math

import jax
import jax.numpy as jnp
from jax import lax
from jax.experimental import pallas as pl
from jax.experimental.pallas import tpu as pltpu
from jax.sharding import PartitionSpec as P

H = 32
KV = 8
HD = 128
LANES = 128
HALF = 32

norm_eps = 1e-06


def block_place(storage, group_rows, block_order):
    block_index = storage // group_rows
    choices_row = jnp.arange(block_order.shape[0], dtype=jnp.int32)
    looked_up = jnp.sum(
        jnp.where(block_index[:, None] == choices_row[None, :], block_order[None, :], 0), axis=1
    )
    return looked_up * group_rows + storage % group_rows


def attention_body(kind_ref, q_ref, kv_ref, qhot_ref, khot_ref, bias_ref, inv_ref, o_ref, qa, ka, acc):
    step = pl.program_id(1)
    group_heads = q_ref.shape[1] // HD
    kind = kind_ref[step]

    @pl.when(step == 0)
    def _():
        acc[...] = jnp.zeros_like(acc)
        for h in range(group_heads):
            qa[h, :, :HD] = q_ref[:, h * HD:(h + 1) * HD]
            qa[h, :, HD:] = (qhot_ref[...] * bias_ref[0, h:h + 1, :]).astype(jnp.bfloat16)

    def tile(diagonal):
        ka[:, :HD] = kv_ref[:, :HD]
        ka[:, HD:] = khot_ref[...]
        for h in range(group_heads):
            half = lax.dot_general(
                qa[h], ka[...], (((1,), (1,)), ((), ())), preferred_element_type=jnp.float32
            )
            w = half * jnp.tanh(half) + half
            if diagonal:
                ti = lax.broadcasted_iota(jnp.int32, w.shape, 0)
                ui = lax.broadcasted_iota(jnp.int32, w.shape, 1)
                w = jnp.where(ui <= ti, w, 0.0)
            acc[h] += jnp.dot(
                w.astype(jnp.bfloat16), kv_ref[:, HD:], preferred_element_type=jnp.float32
            )

    @pl.when(kind == 1)
    def _():
        tile(False)

    @pl.when(kind == 2)
    def _():
        tile(True)

    @pl.when(step == pl.num_programs(1) - 1)
    def _():
        for h in range(group_heads):
            o_ref[:, h * HD:(h + 1) * HD] = (acc[h] * inv_ref[...]).astype(jnp.bfloat16)


def attention(first, groups, kinds, queries, kv_all, query_hot, key_hot, bias_lanes, inv_count):
    rows = queries.shape[0]
    group_heads = bias_lanes.shape[1]
    tiles = kinds.shape[0]
    gw = group_heads * HD
    width = groups * gw
    return pl.pallas_call(
        attention_body,
        grid_spec=pltpu.PrefetchScalarGridSpec(
            num_scalar_prefetch=1,
            grid=(groups, tiles),
            in_specs=[
                pl.BlockSpec((rows, gw), lambda g, j, k: (0, g + first)),
                pl.BlockSpec((rows, 2 * HD), lambda g, j, k: (j, g + first)),
                pl.BlockSpec((rows, LANES), lambda g, j, k: (0, 0)),
                pl.BlockSpec((rows, LANES), lambda g, j, k: (j, 0)),
                pl.BlockSpec((1, group_heads, LANES), lambda g, j, k: (g + first, 0, 0)),
                pl.BlockSpec((rows, 1), lambda g, j, k: (0, 0)),
            ],
            out_specs=pl.BlockSpec((rows, gw), lambda g, j, k: (0, g)),
            scratch_shapes=[
                pltpu.VMEM((group_heads, rows, 2 * HD), jnp.bfloat16),
                pltpu.VMEM((rows, 2 * HD), jnp.bfloat16),
                pltpu.VMEM((group_heads, rows, HD), jnp.float32),
            ],
        ),
        out_shape=jax.ShapeDtypeStruct((rows, width), jnp.bfloat16),
        compiler_params=pltpu.CompilerParams(vmem_limit_bytes=48 * 1024 * 1024),
        cost_estimate=pl.CostEstimate(
            flops=4 * rows * rows * tiles * width, bytes_accessed=rows * tiles * 1024 * 2,
            transcendentals=rows * rows * tiles * width // HD,
        ),
    )(kinds, queries, kv_all, query_hot, key_hot, bias_lanes, inv_count)


MESH = pl.DeviceIdType.MESH
CHUNKS = 4


def partner(index):
    return index + 1 - 2 * (index % 2)


def columns_body(col_count, part, wide, local_sem, send, recv):
    c = lax.axis_index("col")
    peers = [{"col": (c + k) % col_count} for k in range(1, col_count)]
    barrier = pltpu.get_barrier_semaphore()
    for peer in peers:
        pl.semaphore_signal(barrier, inc=1, device_id=peer, device_id_type=MESH)
    pl.semaphore_wait(barrier, len(peers))
    width = part.shape[1]
    size = part.shape[0] // CHUNKS
    columns = pl.ds(pl.multiple_of(c * width, 128), width)
    copies = []
    for i in range(CHUNKS):
        rows = pl.ds(i * size, size)
        for k, peer in enumerate(peers):
            copies.append(pltpu.make_async_remote_copy(
                src_ref=part.at[rows], dst_ref=wide.at[rows, columns],
                send_sem=send.at[k, i], recv_sem=recv.at[k, i],
                device_id=peer, device_id_type=MESH))
    keep = pltpu.make_async_copy(part, wide.at[:, columns], local_sem)
    for copy in copies:
        copy.start()
    keep.start()
    for copy in copies:
        copy.wait()
    keep.wait()


def gather_columns(col_count, part, name):
    dma = pltpu.SemaphoreType.DMA
    return pl.pallas_call(
        functools.partial(columns_body, col_count),
        out_shape=jax.ShapeDtypeStruct((part.shape[0], part.shape[1] * col_count), part.dtype),
        in_specs=[pl.BlockSpec(memory_space=pltpu.VMEM)],
        out_specs=pl.BlockSpec(memory_space=pl.ANY),
        scratch_shapes=[dma, dma((col_count - 1, CHUNKS)), dma((col_count - 1, CHUNKS))],
        compiler_params=pltpu.CompilerParams(
            collective_id=name, has_side_effects=True, vmem_limit_bytes=16 * 1024 * 1024),
        cost_estimate=pl.CostEstimate(
            flops=0, bytes_accessed=32 * part.size * 2, transcendentals=0),
    )(part)


def spread_body(ctx_count, kv, dom, kv_all, dom_all, local_sem,
                up_send, down_send, x_send, c_send, recv_sem):
    z, r = lax.axis_index("ctx"), lax.axis_index("row")
    far, near = (r + 2) % 4, partner(r)
    barrier = pltpu.get_barrier_semaphore()

    def greet(target):
        pl.semaphore_signal(barrier, inc=1, device_id=target, device_id_type=MESH)

    above, below = z < ctx_count - 1, z > 0
    greet({"row": near})
    greet({"row": far})
    pl.when(above)(lambda: greet({"ctx": z + 1}))
    pl.when(below)(lambda: greet({"ctx": z - 1}))
    pl.semaphore_wait(barrier, 2 + (z + ctx_count - 1) // ctx_count + (2 * ctx_count - 2 - z) // ctx_count)

    def copies(zz, rr, send, target, first=False):
        pair = []
        for k, (src, dst) in enumerate(((kv, kv_all), (dom, dom_all))):
            pair.append(pltpu.make_async_remote_copy(
                src_ref=src if first else dst.at[zz, rr], dst_ref=dst.at[zz, rr],
                send_sem=send.at[zz, rr, k],
                recv_sem=recv_sem.at[zz, rr, k], device_id=target, device_id_type=MESH))
        return pair

    def start(pair):
        for copy in pair:
            copy.start()

    def sent(pair):
        for copy in pair:
            copy.wait_send()

    def landed(zz, rr):
        for copy in copies(zz, rr, x_send, {"row": far}):
            copy.wait_recv()

    keep = [pltpu.make_async_copy(kv, kv_all.at[z, r], local_sem.at[0]),
            pltpu.make_async_copy(dom, dom_all.at[z, r], local_sem.at[1])]

    def up(zz, rr, first=False):
        return copies(zz, rr, up_send, {"ctx": z + 1}, first)

    def down(zz, rr, first=False):
        return copies(zz, rr, down_send, {"ctx": z - 1}, first)

    def to_near(zz, rr, first=False):
        return copies(zz, rr, c_send, {"row": near}, first)

    across = copies(z, r, x_send, {"row": far}, True)
    start(across)
    pl.when(above)(lambda: start(up(z, r, True)))
    pl.when(below)(lambda: start(down(z, r, True)))
    start(to_near(z, r, True))
    for copy in keep:
        copy.start()
    landed(z, far)
    pl.when(above)(lambda: start(up(z, far)))
    pl.when(below)(lambda: start(down(z, far)))
    start(to_near(z, far))
    for d in range(1, ctx_count):
        for rr in (r, far):
            @pl.when(z >= d)
            def _():
                landed(z - d, rr)
                pl.when(above)(lambda: start(up(z - d, rr)))
                start(to_near(z - d, rr))

            @pl.when(z + d < ctx_count)
            def _():
                landed(z + d, rr)
                pl.when(below)(lambda: start(down(z + d, rr)))
                start(to_near(z + d, rr))

    sent(across)
    for zz in range(ctx_count):
        landed(zz, near)
        landed(zz, (near + 2) % 4)
        for rr in (r, far):
            sent(to_near(zz, rr))
            pl.when(above & (z >= zz))(lambda zz=zz, rr=rr: sent(up(zz, rr)))
            pl.when(below & (z <= zz))(lambda zz=zz, rr=rr: sent(down(zz, rr)))
    for copy in keep:
        copy.wait()


def gather_keyvals(ctx_count, keyvals, domains, name):
    anywhere = pl.BlockSpec(memory_space=pl.ANY)
    dma = pltpu.SemaphoreType.DMA
    return pl.pallas_call(
        functools.partial(spread_body, ctx_count),
        out_shape=[jax.ShapeDtypeStruct((ctx_count, 4) + keyvals.shape, keyvals.dtype),
                   jax.ShapeDtypeStruct((ctx_count, 4) + domains.shape, domains.dtype)],
        in_specs=[pl.BlockSpec(memory_space=pltpu.VMEM)] * 2,
        out_specs=[anywhere] * 2,
        scratch_shapes=[dma((2,)), dma((ctx_count, 4, 2)), dma((ctx_count, 4, 2)), dma((ctx_count, 4, 2)),
                        dma((ctx_count, 4, 2)), dma((ctx_count, 4, 2))],
        compiler_params=pltpu.CompilerParams(collective_id=name, has_side_effects=True,
                                             vmem_limit_bytes=16 * 1024 * 1024),
        cost_estimate=pl.CostEstimate(
            flops=0, bytes_accessed=128 * keyvals.size * 2, transcendentals=0),
    )(keyvals, domains)


def hot_lanes(domains):
    lane = lax.broadcasted_iota(jnp.int32, (1, LANES), 1)
    return ((lane % HALF == domains[:, None]) & (lane < 2 * HALF)).astype(jnp.bfloat16)


def shards(events, domain_ids, block_order, query_weight, keyval_weight, head_bias, out_weight):
    row_count = events.shape[0]
    head_count = head_bias.shape[0]
    group_size = H // KV
    pair_heads = max(1, head_count // group_size)
    group_heads = head_count // pair_heads
    rows_axis = lax.axis_size("row")
    group_rows = row_count * rows_axis
    scale_factor = 1.0 / math.sqrt(HD)
    col_count = lax.axis_size("col")
    pair_start = lax.axis_index("col") * head_count // group_size
    pair_weight = lax.dynamic_slice_in_dim(keyval_weight, pair_start, pair_heads, 1)
    pair_weight = pair_weight.reshape(keyval_weight.shape[0], pair_heads * 2 * HD)
    pair_all = lax.all_gather(pair_weight, "row", axis=0, tiled=True)
    query_all = lax.all_gather(query_weight, "row", axis=0, tiled=True)
    whole = gather_columns(col_count, events, 1)
    wide_events = whole.astype(jnp.float32)
    normed = (
        wide_events
        * lax.rsqrt(jnp.mean(wide_events * wide_events, axis=1, keepdims=True) + norm_eps)
    ).astype(jnp.bfloat16)
    pair_sums = jnp.dot(
        normed,
        pair_all,
        preferred_element_type=jnp.float32,
    )
    query_sums = jnp.dot(
        normed,
        query_all,
        preferred_element_type=jnp.float32,
    )
    queries = (query_sums * (0.5 * scale_factor)).astype(jnp.bfloat16)
    keyvals = pair_sums.astype(jnp.bfloat16)
    first_row = (lax.axis_index("ctx") * rows_axis + lax.axis_index("row")) * row_count
    query_place = block_place(
        first_row + jnp.arange(row_count, dtype=jnp.int32), group_rows, block_order
    )
    inv_count = lax.rsqrt((query_place + 1).astype(jnp.float32))[:, None]
    half_bias = 0.5 * head_bias
    high = half_bias.astype(jnp.bfloat16).astype(jnp.float32)
    low = half_bias - high
    lane = jnp.arange(LANES, dtype=jnp.int32)[None, :]
    bias_lanes = jnp.where(lane < HALF, high[:, None], jnp.where(lane < 2 * HALF, low[:, None], 0.0))
    bias_lanes = bias_lanes.reshape(pair_heads, group_heads, LANES)
    kv_all, domain_all = gather_keyvals(
        lax.axis_size("ctx"), keyvals, domain_ids.reshape(-1, 128), 2
    )
    kv_all = kv_all.reshape(-1, kv_all.shape[-1])
    domain_all = domain_all.reshape(-1)
    tiles = kv_all.shape[0] // row_count
    tile_first = block_place(
        row_count * jnp.arange(tiles, dtype=jnp.int32), group_rows, block_order
    )
    kinds = jnp.where(
        tile_first < query_place[0], 1, jnp.where(tile_first == query_place[0], 2, 0)
    ).astype(jnp.int32)
    operands = (
        kinds, queries, kv_all, hot_lanes(domain_ids), hot_lanes(domain_all), bias_lanes, inv_count
    )
    if col_count == 2 and pair_heads % 2 == 0:
        groups = pair_heads // 2
        early = attention(0, groups, *operands)
        arrived = lax.ppermute(early, "col", [(0, 1), (1, 0)])
        late_wide = gather_columns(col_count, attention(groups, groups, *operands), 3)
        is_first = lax.axis_index("col") == 0
        width = early.shape[1]
        all_heads = jnp.concatenate(
            [
                jnp.where(is_first, early, arrived),
                late_wide[:, :width],
                jnp.where(is_first, arrived, early),
                late_wide[:, width:],
            ],
            axis=1,
        )
    else:
        all_heads = gather_columns(col_count, attention(0, pair_heads, *operands), 3)
    out_sums = jnp.dot(
        all_heads,
        lax.all_gather(out_weight, "row", axis=0, tiled=True),
        preferred_element_type=jnp.float32,
    )
    return out_sums.astype(jnp.bfloat16)


def solution(mesh):
    in_specs = (
        P(("ctx", "row"), "col"),
        P(("ctx", "row")),
        P(),
        P("row", "col"),
        P("row", None, None, None),
        P("col"),
        P("row", "col"),
    )
    out_specs = P(("ctx", "row"), "col")
    return jax.shard_map(shards, mesh=mesh, in_specs=in_specs, out_specs=out_specs, check_vma=False)
```
